512 devices in a mesh: group: 16 (over y, x_hi), dom: 32 (over x_lo, z, core).
Axes of the slice: x: 4 (x_hi: 2, x_lo: 2; x = x_hi * 2 + x_lo), y: 8, z: 8, core: 2. Of those that a mesh axis runs over, the one named last changes fastest.
Arguments:
- slab: float32 [524288, 400], P(('group', 'dom')), may hold values from -3.5 to 3.5
- row_state: float32 [524288], P(('group', 'dom')), may hold values from 0.001 to 0.1
- relation: float32 [8, 400], replicated, may hold values from 0.5 to 1.5
- lhs_rows: int32 [524288], P(('group', 'dom')), may hold values from 0 to 1023
- rhs_rows: int32 [524288], P(('group', 'dom')), may hold values from 0 to 1023
- rel_ids: int32 [524288], P(('group', 'dom')), may hold values from 0 to 7
- neg_start: int32 [4096], P(('group', 'dom')), may hold values from 0 to 512
- live_edges: int32 [512], P(('group', 'dom')), may hold values from 256 to 1024, as said below
Outputs:
- new_slab: float32 [524288, 400], P(('group', 'dom'))
- new_state: float32 [524288], P(('group', 'dom'))
- rel_grad: float32 [8, 400], replicated
The draws below stay inside these ranges and needn't reach their ends.
Inputs may be any that keep to these rules, and one draw needn't show every extreme that they name: `live_edges`: within 256 to 1024; some partition uses all 1024 slots.
All inputs are finite; a program needn't handle non-finite values.
Results may differ from the reference program's by a relative error of at most 0.0055.
Values may be sent and summed in bfloat16 or wider, within the bound.
No kernel may reach another device: no remote copies, remote signals or barrier semaphores. Data moves between devices by JAX's collectives and lax.ppermute only.
A program may use at most 64 MiB of HBM per device.

```python
import math
import jax
import jax.numpy as jnp
from jax import lax

D = 400
REL = 8
ROWS = 1024
EDGES = 1024
BLOCK = 128
NEG = 512
SWAP_BIT = 1
PARTITIONS = 512
ENTITIES = 524288
EDGES_ALL = 524288
STARTS_ALL = 4096
N_DOM = 32


def draw_slab(key, part):
    key = jax.random.fold_in(key, 11)
    base_scale = D ** (-0.25)
    values = jnp.clip(jax.random.normal(jax.random.fold_in(key, 1), (ENTITIES, D), jnp.float32), -6.0, 6.0) * base_scale
    return jnp.clip(values, -3.5, 3.5).astype(jnp.float32)


def draw_live_edges(key, part):
    key = jax.random.fold_in(key, 23)
    counts = jax.random.randint(jax.random.fold_in(key, 1), (PARTITIONS,), EDGES // 4, EDGES + 1)
    fullest = jax.random.randint(jax.random.fold_in(key, 2), (), 0, PARTITIONS)
    return counts.at[fullest].set(EDGES).astype(jnp.int32)


def place_ends(drawn, rng, least, top_value):
    dims = drawn.shape
    index_at = [jax.random.randint(jax.random.fold_in(rng, axis), (), 0, dims[axis]) for axis in range(len(dims))]
    drawn = drawn.at[tuple(index_at)].set(least)
    longest = dims.index(max(dims))
    index_at[longest] = (index_at[longest] + 1) % dims[longest]
    return drawn.at[tuple(index_at)].set(top_value)


def level_of(stream_key, shape, split, least, high):
    factor_of = 1.0
    for position, blocks in split:
        draws = jax.random.uniform(jax.random.fold_in(jax.random.fold_in(stream_key, 6), position), (blocks,), jnp.float32, least / len(split), high / len(split))
        factor_of = factor_of * jnp.repeat(jnp.exp(draws), shape[position] // blocks).reshape((-1,) + (1,) * (len(shape) - 1 - position))
    return factor_of


def setup_inputs(seed: int = 0) -> dict:
    key_list = jax.random.split(jax.random.key(seed), 9)
    slab = draw_slab(jax.random.fold_in(key_list[8], 71), 0)
    row_state = jnp.clip(jnp.exp(math.log(0.1) - 4.6051702 * jax.random.uniform(key_list[1], (ENTITIES,), jnp.float32) ** level_of(key_list[1], (ENTITIES,), ((0, 512),), -0.2, 0.2)), 0.001, 0.1)
    relation = jnp.clip(jax.random.uniform(key_list[2], (REL, D), jnp.float32, 0.5, 1.5), 0.5, 1.5)
    lhs_rows = place_ends(jax.random.randint(key_list[3], (EDGES_ALL,), 0, ROWS), jax.random.fold_in(key_list[3], 1), 0, ROWS - 1).astype(jnp.int32)
    rhs_rows = place_ends(jax.random.randint(key_list[4], (EDGES_ALL,), 0, ROWS), jax.random.fold_in(key_list[4], 1), 0, ROWS - 1).astype(jnp.int32)
    rel_ids = place_ends(jax.random.randint(key_list[5], (EDGES_ALL,), 0, REL), jax.random.fold_in(key_list[5], 1), 0, REL - 1).astype(jnp.int32)
    neg_start = place_ends(jax.random.randint(key_list[6], (STARTS_ALL,), 0, ROWS - NEG + 1), jax.random.fold_in(key_list[6], 1), 0, ROWS - NEG).astype(jnp.int32)
    live_edges = draw_live_edges(jax.random.fold_in(key_list[8], 71), 0)
    return {"slab": slab, "row_state": row_state, "relation": relation, "lhs_rows": lhs_rows, "rhs_rows": rhs_rows, "rel_ids": rel_ids, "neg_start": neg_start, "live_edges": live_edges}


learn_rate = 0.1

def paired(index):
    group_index = index // N_DOM
    within = index % N_DOM
    stride = 2 ** SWAP_BIT
    bitval = group_index // stride % 2
    return ((group_index + stride - 2 * stride * bitval) * N_DOM + within).astype(jnp.int32)

def block_terms(target_slab, queries, targets, starts, weights):
    blocks = queries.shape[0] // BLOCK
    width = queries.shape[1]

    def step(carry, items):
        query_block, target_block, start, weight_block = items
        negatives = lax.dynamic_slice_in_dim(target_slab, start, NEG, 0)
        positives = target_slab[target_block]
        pos = lax.optimization_barrier(jnp.sum(query_block.astype(jnp.float32) * positives.astype(jnp.float32), axis=1))
        neg = lax.dot_general(query_block, negatives, (((1,), (1,)), ((), ())), preferred_element_type=jnp.float32)
        top = jnp.maximum(lax.optimization_barrier(jnp.max(neg, axis=1)), pos)
        pos_exp = jnp.exp(pos - top)
        neg_exp = jnp.exp(neg - top[:, None])
        total = pos_exp + lax.optimization_barrier(jnp.sum(neg_exp, axis=1))
        gpos = weight_block * (pos_exp / total - 1.0)
        gneg = (weight_block[:, None] * neg_exp / total[:, None]).astype(jnp.bfloat16)
        dquery = gpos[:, None] * positives.astype(jnp.float32) + jnp.dot(gneg, negatives, preferred_element_type=jnp.float32)
        dneg = lax.dot_general(gneg, query_block, (((0,), (0,)), ((), ())), preferred_element_type=jnp.float32)
        window = lax.dynamic_slice_in_dim(carry, start, NEG, 0)
        carry = lax.dynamic_update_slice_in_dim(carry, window + dneg, start, 0)
        carry = carry.at[target_block].add(gpos[:, None] * query_block.astype(jnp.float32))
        return (carry, dquery)
    start_grad = jnp.zeros((target_slab.shape[0], width), jnp.float32)
    items = (queries.reshape(blocks, BLOCK, width), targets.reshape(blocks, BLOCK), starts, weights.reshape(blocks, BLOCK))
    target_grad, dquery = lax.scan(step, start_grad, items)
    return (dquery.reshape(blocks * BLOCK, width), target_grad)

def make_queries(own_slab, relation, sources, kinds):
    onehot = (kinds[None, :] == jnp.arange(relation.shape[0], dtype=jnp.int32)[:, None]).astype(jnp.float32)
    rel_rows = lax.dot_general(onehot, relation, (((0,), (0,)), ((), ())), precision=lax.Precision.HIGHEST, preferred_element_type=jnp.float32)
    source_vecs = own_slab[sources].astype(jnp.float32)
    return (onehot, rel_rows, source_vecs, (source_vecs * rel_rows).astype(jnp.bfloat16))

def reference(slab, row_state, relation, lhs_rows, rhs_rows, rel_ids, neg_start, live_edges):
    embed = slab.astype(jnp.bfloat16).reshape(PARTITIONS, ROWS, D)
    partner = paired(jnp.arange(PARTITIONS, dtype=jnp.int32))
    blocks = EDGES // BLOCK

    def per_partition(index):
        own_slab = embed[index]
        other_slab = embed[partner[index]]
        sources = lax.dynamic_slice_in_dim(lhs_rows, index * EDGES, EDGES)
        targets = lax.dynamic_slice_in_dim(rhs_rows, index * EDGES, EDGES)
        kinds = lax.dynamic_slice_in_dim(rel_ids, index * EDGES, EDGES)
        starts = lax.dynamic_slice_in_dim(neg_start, index * blocks, blocks)
        weights = (jnp.arange(EDGES, dtype=jnp.int32) < live_edges[index]).astype(jnp.float32)
        onehot, rel_rows, source_vecs, queries = make_queries(own_slab, relation, sources, kinds)
        dquery, other_grad = block_terms(other_slab, queries, targets, starts, weights)
        own_grad = jnp.zeros((ROWS, D), jnp.float32).at[sources].add(dquery * rel_rows)
        rel_part = jnp.dot(onehot, dquery * source_vecs, precision=lax.Precision.HIGHEST, preferred_element_type=jnp.float32)
        return (own_grad, other_grad, rel_part)
    own_grads, other_grads, rel_parts = lax.map(per_partition, jnp.arange(PARTITIONS, dtype=jnp.int32))
    grad = own_grads + other_grads[partner]
    state = row_state.reshape(PARTITIONS, ROWS) + lax.optimization_barrier(jnp.mean(grad * grad, axis=2))
    updated = slab.reshape(PARTITIONS, ROWS, D) - learn_rate * grad / jnp.sqrt(state)[:, :, None]
    rel_grad = lax.optimization_barrier(jnp.sum(rel_parts, axis=0)) / jnp.sqrt(jnp.float32(EDGES_ALL))
    return (updated.reshape(ENTITIES, D), state.reshape(ENTITIES), rel_grad)
```

```python
import jax
import jax.numpy as jnp
from jax import lax
from jax.experimental import pallas as pl
from jax.experimental.pallas import tpu as pltpu
from jax.sharding import Mesh
from jax.sharding import PartitionSpec as P

BLOCK = 128
NEG = 512
AXES = ("y", "x_hi", "x_lo", "z", "core")
TILE = 256

learn_rate = 0.1

NN = (((1,), (0,)), ((), ()))
NT = (((1,), (1,)), ((), ()))
TN = (((0,), (0,)), ((), ()))


def swapped(x):
    return lax.ppermute(x, "y", [(i, i ^ 1) for i in range(lax.axis_size("y"))])


def summed(x, axes):
    terms = jnp.broadcast_to(x[None], (lax.axis_size(axes),) + x.shape)
    return jnp.sum(lax.all_to_all(terms, axes, 0, 0), axis=0)


def dot(a, b, dims):
    return lax.dot_general(a, b, dims, preferred_element_type=jnp.float32)


def split(x):
    high = x.astype(jnp.bfloat16)
    return high, (x - high.astype(jnp.float32)).astype(jnp.bfloat16)


def prepare_kernel(
    starts, live, embed, relation, lhs, rhs, kinds, source, rel_rows, query, query_rows, counts, target, target_grad
):
    rows, edges = embed.shape[1], lhs.shape[1]
    kind_hot = lax.broadcasted_iota(jnp.int32, (relation.shape[0], edges), 0) == kinds[...]
    rel_rows[...] = lax.dot_general(
        relation[...],
        kind_hot.astype(jnp.float32),
        TN,
        precision=lax.Precision.HIGHEST,
        preferred_element_type=jnp.float32,
    )
    for at in range(0, edges, TILE):
        here = slice(at, at + TILE)
        left_hot = lax.broadcasted_iota(jnp.int32, (rows, TILE), 0) == lhs[:, here]
        source[:, here] = dot(
            embed[...], left_hot.astype(jnp.float32).astype(jnp.bfloat16), NN
        )
        query_here = source[:, here] * rel_rows[:, here]
        query[:, here] = query_here.astype(jnp.bfloat16)
        query_rows[here, :] = query_here.T.astype(jnp.bfloat16)
    row = lax.broadcasted_iota(jnp.int32, (BLOCK, rows), 1)
    for block in range(edges // BLOCK):
        here = slice(block * BLOCK, (block + 1) * BLOCK)
        index = jnp.broadcast_to(rhs[:, here].astype(jnp.float32), (BLOCK, BLOCK)).T
        index = jnp.concatenate([index] * (rows // BLOCK), axis=1).astype(jnp.int32)
        slot = lax.broadcasted_iota(jnp.int32, (BLOCK, rows), 0) + block * BLOCK
        right_hot = (row == index).astype(jnp.float32)
        begin = starts[block]
        window = ((row >= begin) & (row < begin + NEG)).astype(jnp.float32)
        counts[here, :] = (window + right_hot).astype(jnp.bfloat16)
        target[here, :] = jnp.where(slot < live[0], right_hot, 0.0).astype(jnp.bfloat16)
    target_grad[...] = -dot(query[...], target[...], NN)


def score_kernel(live, other, query, query_rows, counts, target_grad, softmax, sent_grad):
    edges = query.shape[1]
    total_grad = target_grad[...]
    for at in range(0, edges, TILE):
        here = slice(at, at + TILE)
        count = counts[here, :].astype(jnp.float32)
        score = jnp.where(count > 0.0, dot(query_rows[here, :], other[...], NN), -1e30)
        top = jnp.max(score, axis=1, keepdims=True)
        power = jnp.exp(score - top) * count
        total = jnp.sum(power, axis=1, keepdims=True)
        slot = lax.broadcasted_iota(jnp.int32, total.shape, 0) + at
        weight = jnp.where(slot < live[0], 1.0, 0.0) / total
        softmax[here, :] = (power * weight).astype(jnp.bfloat16)
        total_grad = total_grad + dot(query[:, here], softmax[here, :], NN)
    sent_grad[...] = total_grad.astype(jnp.bfloat16)


def relation_kernel(other, softmax, target, source, rel_rows, kinds, rel_part, left_grad):
    edges = kinds.shape[1]
    part = jnp.zeros(rel_part.shape, jnp.float32)
    for at in range(0, edges, TILE):
        here = slice(at, at + TILE)
        dquery = dot(other[...], softmax[here, :], NT) - dot(other[...], target[here, :], NT)
        kind_hot = lax.broadcasted_iota(jnp.int32, (rel_part.shape[0], TILE), 0) == kinds[:, here]
        kind_hot = kind_hot.astype(jnp.float32).astype(jnp.bfloat16)
        high, low = split(dquery * source[:, here])
        part = part + dot(kind_hot, high, NT) + dot(kind_hot, low, NT)
        left_grad[:, here] = (dquery * rel_rows[:, here]).astype(jnp.bfloat16)
    rel_part[...] = part


def update_kernel(slab, state, left_grad, lhs, received, new_slab, new_state):
    rows, edges = slab.shape[1], lhs.shape[1]
    grad = received[...].astype(jnp.float32)
    for at in range(0, edges, TILE):
        here = slice(at, at + TILE)
        left_hot = lax.broadcasted_iota(jnp.int32, (rows, TILE), 0) == lhs[:, here]
        grad = grad + dot(left_grad[:, here], left_hot.astype(jnp.float32).astype(jnp.bfloat16), NT)
    total = state[...] + jnp.sum(grad * grad, axis=0, keepdims=True) * (1.0 / grad.shape[0])
    new_state[...] = total
    new_slab[...] = slab[...] - grad * (learn_rate / jnp.sqrt(total))


def call(kernel, outs, scalars, vectors, flops):
    scalar = pl.BlockSpec(memory_space=pltpu.SMEM)
    vector = pl.BlockSpec(memory_space=pltpu.VMEM)
    return pl.pallas_call(
        kernel,
        out_shape=[jax.ShapeDtypeStruct(shape, dtype) for shape, dtype in outs],
        in_specs=[scalar] * len(scalars) + [vector] * len(vectors),
        out_specs=[vector] * len(outs),
        compiler_params=pltpu.CompilerParams(vmem_limit_bytes=48 * 2**20),
        cost_estimate=pl.CostEstimate(flops=flops, bytes_accessed=8 * 2**20, transcendentals=0),
    )(*scalars, *vectors)


def on_device(slab, row_state, relation, lhs_rows, rhs_rows, rel_ids, neg_start, live_edges):
    rows, width = slab.shape
    edges = lhs_rows.shape[0]
    bf16, f32 = jnp.bfloat16, jnp.float32
    columns = slab.T
    embed = columns.astype(bf16)
    other = swapped(embed)
    lhs, rhs, kinds = (x.reshape(1, edges) for x in (lhs_rows, rhs_rows, rel_ids))
    work = 2 * rows * edges * width
    source, rel_rows, query, query_rows, counts, target, target_grad = call(
        prepare_kernel,
        [
            ((width, edges), f32),
            ((width, edges), f32),
            ((width, edges), bf16),
            ((edges, width), bf16),
            ((edges, rows), bf16),
            ((edges, rows), bf16),
            ((width, rows), f32),
        ],
        (neg_start, live_edges),
        (embed, relation, lhs, rhs, kinds),
        2 * work,
    )
    softmax, sent_grad = call(
        score_kernel,
        [((edges, rows), bf16), ((width, rows), bf16)],
        (live_edges,),
        (other, query, query_rows, counts, target_grad),
        2 * work,
    )
    received = swapped(sent_grad)
    rel_part, left_grad = call(
        relation_kernel,
        [(relation.shape, f32), ((width, edges), bf16)],
        (),
        (other, softmax, target, source, rel_rows, kinds),
        3 * work,
    )
    rel_total = summed(summed(summed(rel_part, ("z", "core")), ("x_hi", "x_lo")), "y")
    edge_total = edges * lax.axis_size(AXES)
    rel_grad = rel_total / jnp.sqrt(jnp.float32(edge_total))
    new_columns, new_state = call(
        update_kernel,
        [((width, rows), f32), ((1, rows), f32)],
        (),
        (columns, row_state.reshape(1, rows), left_grad, lhs, received),
        work,
    )
    return (new_columns.T, new_state.reshape(rows), rel_grad)


def solution(mesh):
    group, dom = mesh.devices.shape
    fine = Mesh(mesh.devices.reshape(group // 2, 2, 2, dom // 4, 2), AXES)
    split_rows, split = P(AXES, None), P(AXES)
    in_specs = (split_rows, split, P(), split, split, split, split, split)
    out_specs = (split_rows, split, P())
    return jax.shard_map(
        on_device, mesh=fine, in_specs=in_specs, out_specs=out_specs, check_vma=False
    )
```

```python
import functools
import math

import jax
import jax.numpy as jnp
import numpy as np
from jax import lax
from jax.experimental import pallas as pl
from jax.experimental.pallas import tpu as pltpu
from jax.sharding import Mesh
from jax.sharding import PartitionSpec as P

BLOCK = 128
NEG = 512
AXES = ("y", "x_hi", "x_lo", "z", "core")
NEAR = ("x_hi", "x_lo", "z", "core")
FAR = ("y", "x_lo", "core")
PIECE = 128
TILE = 256
WIDE = 512
CUT = 512
LOG_TWO = 0.6931471805599453
NEVER = -1e30

learn_rate = 0.1

NN = (((1,), (0,)), ((), ()))
NT = (((1,), (1,)), ((), ()))
TN = (((0,), (0,)), ((), ()))


def axis_size(axes):
    return lax.axis_size(axes)


def swapped(x):
    return lax.ppermute(x, "y", [(i, i ^ 1) for i in range(lax.axis_size("y"))])


def exchanged(terms, axes):
    return lax.all_to_all(terms, axes, 0, 0)


def pieces(axes):
    place = np.indices([axis_size(axis) for axis in axes]).reshape(len(axes), -1)
    return [int(k) for k in place[axes.index("x_lo")] * 2 + place[axes.index("core")]]


def dot(a, b, dims):
    return lax.dot_general(a, b, dims, preferred_element_type=jnp.float32)


def split(x):
    high = x.astype(jnp.bfloat16)
    return high, (x - high.astype(jnp.float32)).astype(jnp.bfloat16)


def one_hot(index, classes):
    row = lax.broadcasted_iota(jnp.int32, (classes, index.shape[1]), 0)
    return (row == index).astype(jnp.float32)


def prepare_kernel(starts, live, embed, relation, lhs, rhs, kinds, source, rel_rows, query, query_rows, bias, target, target_grad):
    rows, edges = embed.shape[1], lhs.shape[1]
    rel_rows[...] = lax.dot_general(
        relation[...],
        one_hot(kinds[...], relation.shape[0]),
        TN,
        precision=lax.Precision.HIGHEST,
        preferred_element_type=jnp.float32,
    )
    for at in range(0, edges, TILE):
        here = slice(at, at + TILE)
        source_here = dot(embed[...], one_hot(lhs[:, here], rows).astype(jnp.bfloat16), NN)
        query_here = source_here * rel_rows[:, here]
        source[:, here] = source_here.astype(jnp.bfloat16)
        query[:, here] = query_here.astype(jnp.bfloat16)
        query_rows[here, :] = query_here.T.astype(jnp.bfloat16)
    row = lax.broadcasted_iota(jnp.int32, (BLOCK, rows), 1)
    for block in range(edges // BLOCK):
        here = slice(block * BLOCK, (block + 1) * BLOCK)
        index = jnp.broadcast_to(rhs[:, here].astype(jnp.float32), (BLOCK, BLOCK)).T
        index = jnp.concatenate([index] * (rows // BLOCK), axis=1).astype(jnp.int32)
        slot = lax.broadcasted_iota(jnp.int32, (BLOCK, rows), 0) + block * BLOCK
        is_target = row == index
        begin = starts[block]
        in_window = (row >= begin) & (row < begin + NEG)
        bias[here, :] = jnp.where(
            in_window, jnp.where(is_target, LOG_TWO, 0.0), jnp.where(is_target, 0.0, NEVER)
        )
        target[here, :] = jnp.where(is_target & (slot < live[0]), 1.0, 0.0).astype(jnp.bfloat16)
    target_grad[...] = -dot(query[...], target[...], NN)


def first_kernel(other, query_rows, bias, target, power, top, total, positives):
    edges, cut = bias.shape[0], other.shape[1]
    for at in range(0, edges, TILE):
        here = slice(at, at + TILE)
        score = dot(query_rows[here, :], other[...], NN) + bias[here, :cut]
        top_here = jnp.max(score, axis=1, keepdims=True)
        power_here = jnp.exp(score - top_here)
        power[here, :] = power_here
        top[here, :] = top_here
        total[here, :] = jnp.sum(power_here, axis=1, keepdims=True)
        positives[:, here] = dot(other[...], target[here, :cut], NT)


def second_kernel(
    live, rest, query, query_rows, bias, target_grad, power, top, total, softmax, sent_grad
):
    edges, cut = power.shape
    for at in range(0, edges, TILE):
        here = slice(at, at + TILE)
        score = dot(query_rows[here, :], rest[...], NN) + bias[here, cut:]
        top_here = jnp.maximum(jnp.max(score, axis=1, keepdims=True), top[here, :])
        power_here = jnp.exp(score - top_here)
        scale = jnp.exp(top[here, :] - top_here)
        total_here = jnp.sum(power_here, axis=1, keepdims=True) + total[here, :] * scale
        slot = lax.broadcasted_iota(jnp.int32, total_here.shape, 0) + at
        weight = jnp.where(slot < live[0], 1.0, 0.0) / total_here
        softmax[here, :cut] = (power[here, :] * (scale * weight)).astype(jnp.bfloat16)
        softmax[here, cut:] = (power_here * weight).astype(jnp.bfloat16)
    sent_grad[...] = (target_grad[...] + dot(query[...], softmax[...], NN)).astype(jnp.bfloat16)


def relation_kernel(
    near_pieces, other, rest, softmax, target, positives, source, rel_rows, kinds, left_grad, terms
):
    edges, cut = softmax.shape[0], other.shape[1]
    part = jnp.zeros((source.shape[0], terms.shape[1]), jnp.float32)
    for at in range(0, edges, WIDE):
        here = slice(at, at + WIDE)
        dquery = (
            dot(other[...], softmax[here, :cut], NT)
            + dot(rest[...], softmax[here, cut:], NT)
            - dot(rest[...], target[here, cut:], NT)
            - positives[:, here]
        )
        kind_hot = one_hot(kinds[:, here], part.shape[1]).astype(jnp.bfloat16)
        high, low = split(dquery * source[:, here].astype(jnp.float32))
        part = part + (dot(high, kind_hot, NT) + dot(low, kind_hot, NT))
        left_grad[:, here] = (dquery * rel_rows[:, here]).astype(jnp.bfloat16)
    part = part.T
    part = jnp.concatenate([part, jnp.zeros((part.shape[0], -part.shape[1] % PIECE), part.dtype)], axis=1)
    part = part.astype(terms.dtype)
    for k, piece in enumerate(near_pieces):
        terms[k] = part[:, piece * PIECE : (piece + 1) * PIECE]


def pass_on_kernel(terms, summed):
    total = terms[0].astype(jnp.float32)
    for k in range(1, terms.shape[0]):
        total = total + terms[k].astype(jnp.float32)
    total = total.astype(summed.dtype)
    for k in range(summed.shape[0]):
        summed[k] = total


def collect_kernel(far_pieces, scale, terms, rel_grad):
    width = rel_grad.shape[1]
    total = {}
    for k, piece in enumerate(far_pieces):
        term = terms[k].astype(jnp.float32)
        total[piece] = total[piece] + term if piece in total else term
    for piece, term in total.items():
        end = min(width, (piece + 1) * PIECE)
        rel_grad[:, piece * PIECE : end] = term[:, : end - piece * PIECE] * scale


def source_kernel(left_grad, lhs, source_grad):
    edges, rows = lhs.shape[1], source_grad.shape[1]
    grad = jnp.zeros(source_grad.shape, jnp.float32)
    for at in range(0, edges, TILE):
        here = slice(at, at + TILE)
        grad = grad + dot(left_grad[:, here], one_hot(lhs[:, here], rows).astype(jnp.bfloat16), NT)
    source_grad[...] = grad


def update_kernel(slab, state, source_grad, received, new_slab, new_state):
    grad = source_grad[...] + received[...].astype(jnp.float32)
    total = state[...] + jnp.sum(grad * grad, axis=0, keepdims=True) * (1.0 / grad.shape[0])
    new_state[...] = total
    new_slab[...] = slab[...] - grad * (learn_rate / jnp.sqrt(total))


def call(kernel, outs, scalars, vectors, flops, scratch=()):
    scalar = pl.BlockSpec(memory_space=pltpu.SMEM)
    vector = pl.BlockSpec(memory_space=pltpu.VMEM)
    return pl.pallas_call(
        kernel,
        out_shape=[jax.ShapeDtypeStruct(shape, dtype) for shape, dtype in outs],
        in_specs=[scalar] * len(scalars) + [vector] * len(vectors),
        out_specs=[vector] * len(outs),
        scratch_shapes=[pltpu.VMEM(shape, dtype) for shape, dtype in scratch],
        compiler_params=pltpu.CompilerParams(vmem_limit_bytes=24 * 2**20),
        cost_estimate=pl.CostEstimate(flops=flops, bytes_accessed=8 * 2**20, transcendentals=0),
    )(*scalars, *vectors)


def on_device(slab, row_state, relation, lhs_rows, rhs_rows, rel_ids, neg_start, live_edges):
    rows, width = slab.shape
    edges = lhs_rows.shape[0]
    bf16, f32 = jnp.bfloat16, jnp.float32
    columns = slab.T
    embed = columns.astype(bf16)
    other, rest = swapped(embed[:, :CUT]), swapped(embed[:, CUT:])
    lhs, rhs, kinds = (x.reshape(1, edges) for x in (lhs_rows, rhs_rows, rel_ids))
    work = 2 * rows * edges * width
    source, rel_rows, query, query_rows, bias, target, target_grad = call(
        prepare_kernel,
        [
            ((width, edges), bf16),
            ((width, edges), f32),
            ((width, edges), bf16),
            ((edges, width), bf16),
            ((edges, rows), f32),
            ((edges, rows), bf16),
            ((width, rows), f32),
        ],
        (neg_start, live_edges),
        (embed, relation, lhs, rhs, kinds),
        2 * work,
    )
    power, top, total, positives = call(
        first_kernel,
        [((edges, CUT), f32), ((edges, 1), f32), ((edges, 1), f32), ((width, edges), f32)],
        (),
        (other, query_rows, bias, target),
        work,
    )
    softmax, sent_grad = call(
        second_kernel,
        [((edges, rows), bf16), ((width, rows), bf16)],
        (live_edges,),
        (rest, query, query_rows, bias, target_grad, power, top, total),
        2 * work,
    )
    received = swapped(sent_grad)
    near, far = pieces(NEAR), pieces(FAR)
    piece = (relation.shape[0], PIECE)
    left_grad, terms = call(
        functools.partial(relation_kernel, near),
        [((width, edges), bf16), ((len(near),) + piece, bf16)],
        (),
        (other, rest, softmax, target, positives, source, rel_rows, kinds),
        2 * work,
    )
    terms = exchanged(terms, NEAR)
    (source_grad,) = call(
        source_kernel,
        [((width, rows), f32)],
        (),
        (left_grad, lhs),
        work,
    )
    (terms,) = call(pass_on_kernel, [((len(far),) + piece, bf16)], (), (terms,), 10**5)
    received, terms = lax.optimization_barrier((received, terms))
    terms = exchanged(terms, FAR)
    new_columns, new_state = call(
        update_kernel,
        [((width, rows), f32), ((1, rows), f32)],
        (),
        (columns, row_state.reshape(1, rows), source_grad, received),
        work // 100,
    )
    new_state, terms = lax.optimization_barrier((new_state, terms))
    scale = 1.0 / math.sqrt(edges * axis_size(AXES))
    (rel_grad,) = call(
        functools.partial(collect_kernel, far, scale), [(relation.shape, f32)], (), (terms,), 10**5
    )
    return (new_columns.T, new_state.reshape(rows), rel_grad)


def solution(mesh):
    group, dom = mesh.devices.shape
    fine = Mesh(mesh.devices.reshape(group // 2, 2, 2, dom // 4, 2), AXES)
    split_rows, split = P(AXES, None), P(AXES)
    in_specs = (split_rows, split, P(), split, split, split, split, split)
    out_specs = (split_rows, split, P())
    return jax.shard_map(
        on_device, mesh=fine, in_specs=in_specs, out_specs=out_specs, check_vma=False
    )
```

```python
import functools
import math

import jax
import jax.numpy as jnp
import numpy as np
from jax import lax
from jax.experimental import pallas as pl
from jax.experimental.pallas import tpu as pltpu
from jax.sharding import Mesh
from jax.sharding import PartitionSpec as P

BLOCK = 128
NEG = 512
AXES = ("y", "x_hi", "x_lo", "z", "core")
NEAR = ("x_hi", "x_lo", "z", "core")
FAR = ("y", "x_lo", "core")
PIECE = 128
TILE = 256
WIDE = 512
CUT = 768
LOG_TWO = 0.6931471805599453
NEVER = -1e30

learn_rate = 0.1

NN = (((1,), (0,)), ((), ()))
NT = (((1,), (1,)), ((), ()))
TN = (((0,), (0,)), ((), ()))


def axis_size(axes):
    return lax.axis_size(axes)


def swapped(x):
    return lax.ppermute(x, "y", [(i, i ^ 1) for i in range(lax.axis_size("y"))])


def exchanged(terms, axes):
    return lax.all_to_all(terms, axes, 0, 0)


def pieces(axes):
    place = np.indices([axis_size(axis) for axis in axes]).reshape(len(axes), -1)
    return [int(k) for k in place[axes.index("x_lo")] * 2 + place[axes.index("core")]]


def dot(a, b, dims):
    return lax.dot_general(a, b, dims, preferred_element_type=jnp.float32)


def split(x):
    high = x.astype(jnp.bfloat16)
    return high, (x - high.astype(jnp.float32)).astype(jnp.bfloat16)


def one_hot(index, classes):
    row = lax.broadcasted_iota(jnp.int32, (classes, index.shape[1]), 0)
    return (row == index).astype(jnp.float32)


def prepare_kernel(starts, live, embed, embed_rest, relation, lhs, rhs, kinds, source, rel_rows, query, query_rows, bias, target, target_grad):
    cut, rows, edges = embed.shape[1], target.shape[1], lhs.shape[1]
    rel_rows[...] = lax.dot_general(
        relation[...],
        one_hot(kinds[...], relation.shape[0]),
        TN,
        precision=lax.Precision.HIGHEST,
        preferred_element_type=jnp.float32,
    )
    for at in range(0, edges, TILE):
        here = slice(at, at + TILE)
        left_hot = one_hot(lhs[:, here], rows).astype(jnp.bfloat16)
        source_here = dot(embed[...], left_hot[:cut, :], NN) + dot(embed_rest[...], left_hot[cut:, :], NN)
        query_here = source_here * rel_rows[:, here]
        source[:, here] = source_here.astype(jnp.bfloat16)
        query[:, here] = query_here.astype(jnp.bfloat16)
        query_rows[here, :] = query_here.T.astype(jnp.bfloat16)
    row = lax.broadcasted_iota(jnp.int32, (BLOCK, rows), 1)
    for block in range(edges // BLOCK):
        here = slice(block * BLOCK, (block + 1) * BLOCK)
        index = jnp.broadcast_to(rhs[:, here].astype(jnp.float32), (BLOCK, BLOCK)).T
        index = jnp.concatenate([index] * (rows // BLOCK), axis=1).astype(jnp.int32)
        slot = lax.broadcasted_iota(jnp.int32, (BLOCK, rows), 0) + block * BLOCK
        is_target = row == index
        begin = starts[block]
        in_window = (row >= begin) & (row < begin + NEG)
        bias[here, :] = jnp.where(
            in_window, jnp.where(is_target, LOG_TWO, 0.0), jnp.where(is_target, 0.0, NEVER)
        )
        target[here, :] = jnp.where(is_target & (slot < live[0]), 1.0, 0.0).astype(jnp.bfloat16)
    target_grad[...] = -dot(query[...], target[...], NN)


def first_kernel(other, query_rows, bias, target, power, top, total, positives):
    edges, cut = bias.shape[0], other.shape[1]
    for at in range(0, edges, TILE):
        here = slice(at, at + TILE)
        score = dot(query_rows[here, :], other[...], NN) + bias[here, :cut]
        top_here = jnp.max(score, axis=1, keepdims=True)
        power_here = jnp.exp(score - top_here)
        power[here, :] = power_here
        top[here, :] = top_here
        total[here, :] = jnp.sum(power_here, axis=1, keepdims=True)
        positives[:, here] = dot(other[...], target[here, :cut], NT)


def second_kernel(
    live, rest, query, query_rows, bias, target_grad, power, top, total, softmax, sent_grad
):
    edges, cut = power.shape
    for at in range(0, edges, TILE):
        here = slice(at, at + TILE)
        score = dot(query_rows[here, :], rest[...], NN) + bias[here, cut:]
        top_here = jnp.maximum(jnp.max(score, axis=1, keepdims=True), top[here, :])
        power_here = jnp.exp(score - top_here)
        scale = jnp.exp(top[here, :] - top_here)
        total_here = jnp.sum(power_here, axis=1, keepdims=True) + total[here, :] * scale
        slot = lax.broadcasted_iota(jnp.int32, total_here.shape, 0) + at
        weight = jnp.where(slot < live[0], 1.0, 0.0) / total_here
        softmax[here, :cut] = (power[here, :] * (scale * weight)).astype(jnp.bfloat16)
        softmax[here, cut:] = (power_here * weight).astype(jnp.bfloat16)
    sent_grad[...] = (target_grad[...] + dot(query[...], softmax[...], NN)).astype(jnp.bfloat16)


def relation_kernel(
    near_pieces, other, rest, softmax, target, positives, source, rel_rows, kinds, left_grad, terms
):
    edges, cut = softmax.shape[0], other.shape[1]
    part = jnp.zeros((source.shape[0], terms.shape[1]), jnp.float32)
    for at in range(0, edges, WIDE):
        here = slice(at, at + WIDE)
        dquery = (
            dot(other[...], softmax[here, :cut], NT)
            + dot(rest[...], softmax[here, cut:], NT)
            - dot(rest[...], target[here, cut:], NT)
            - positives[:, here]
        )
        kind_hot = one_hot(kinds[:, here], part.shape[1]).astype(jnp.bfloat16)
        high, low = split(dquery * source[:, here].astype(jnp.float32))
        part = part + (dot(high, kind_hot, NT) + dot(low, kind_hot, NT))
        left_grad[:, here] = (dquery * rel_rows[:, here]).astype(jnp.bfloat16)
    part = part.T
    part = jnp.concatenate([part, jnp.zeros((part.shape[0], -part.shape[1] % PIECE), part.dtype)], axis=1)
    part = part.astype(terms.dtype)
    for k, piece in enumerate(near_pieces):
        terms[k] = part[:, piece * PIECE : (piece + 1) * PIECE]


def pass_on_kernel(terms, summed):
    total = terms[0].astype(jnp.float32)
    for k in range(1, terms.shape[0]):
        total = total + terms[k].astype(jnp.float32)
    total = total.astype(summed.dtype)
    for k in range(summed.shape[0]):
        summed[k] = total


def collect_kernel(far_pieces, scale, terms, rel_grad):
    width = rel_grad.shape[1]
    total = {}
    for k, piece in enumerate(far_pieces):
        term = terms[k].astype(jnp.float32)
        total[piece] = total[piece] + term if piece in total else term
    for piece, term in total.items():
        end = min(width, (piece + 1) * PIECE)
        rel_grad[:, piece * PIECE : end] = term[:, : end - piece * PIECE] * scale


def source_kernel(left_grad, lhs, source_grad):
    edges, rows = lhs.shape[1], source_grad.shape[1]
    grad = jnp.zeros(source_grad.shape, jnp.float32)
    for at in range(0, edges, TILE):
        here = slice(at, at + TILE)
        grad = grad + dot(left_grad[:, here], one_hot(lhs[:, here], rows).astype(jnp.bfloat16), NT)
    source_grad[...] = grad


def update_kernel(slab, state, source_grad, received, new_slab, new_state):
    grad = source_grad[...] + received[...].astype(jnp.float32)
    total = state[...] + jnp.sum(grad * grad, axis=0, keepdims=True) * (1.0 / grad.shape[0])
    new_state[...] = total
    new_slab[...] = slab[...] - grad * (learn_rate / jnp.sqrt(total))


def call(kernel, outs, scalars, vectors, flops, scratch=()):
    scalar = pl.BlockSpec(memory_space=pltpu.SMEM)
    vector = pl.BlockSpec(memory_space=pltpu.VMEM)
    return pl.pallas_call(
        kernel,
        out_shape=[jax.ShapeDtypeStruct(shape, dtype) for shape, dtype in outs],
        in_specs=[scalar] * len(scalars) + [vector] * len(vectors),
        out_specs=[vector] * len(outs),
        scratch_shapes=[pltpu.VMEM(shape, dtype) for shape, dtype in scratch],
        compiler_params=pltpu.CompilerParams(vmem_limit_bytes=24 * 2**20),
        cost_estimate=pl.CostEstimate(flops=flops, bytes_accessed=8 * 2**20, transcendentals=0),
    )(*scalars, *vectors)


def on_device(slab, row_state, relation, lhs_rows, rhs_rows, rel_ids, neg_start, live_edges):
    rows, width = slab.shape
    edges = lhs_rows.shape[0]
    bf16, f32 = jnp.bfloat16, jnp.float32
    columns = slab.T
    embed = columns[:, :CUT].astype(bf16)
    other = swapped(embed)
    embed, later = lax.optimization_barrier((embed, columns[:, CUT:]))
    embed_rest = later.astype(bf16)
    rest = swapped(embed_rest)
    lhs, rhs, kinds = (x.reshape(1, edges) for x in (lhs_rows, rhs_rows, rel_ids))
    work = 2 * rows * edges * width
    source, rel_rows, query, query_rows, bias, target, target_grad = call(
        prepare_kernel,
        [
            ((width, edges), bf16),
            ((width, edges), f32),
            ((width, edges), bf16),
            ((edges, width), bf16),
            ((edges, rows), f32),
            ((edges, rows), bf16),
            ((width, rows), f32),
        ],
        (neg_start, live_edges),
        (embed, embed_rest, relation, lhs, rhs, kinds),
        2 * work,
    )
    power, top, total, positives = call(
        first_kernel,
        [((edges, CUT), f32), ((edges, 1), f32), ((edges, 1), f32), ((width, edges), f32)],
        (),
        (other, query_rows, bias, target),
        work,
    )
    softmax, sent_grad = call(
        second_kernel,
        [((edges, rows), bf16), ((width, rows), bf16)],
        (live_edges,),
        (rest, query, query_rows, bias, target_grad, power, top, total),
        2 * work,
    )
    received = swapped(sent_grad)
    near, far = pieces(NEAR), pieces(FAR)
    piece = (relation.shape[0], PIECE)
    left_grad, terms = call(
        functools.partial(relation_kernel, near),
        [((width, edges), bf16), ((len(near),) + piece, bf16)],
        (),
        (other, rest, softmax, target, positives, source, rel_rows, kinds),
        2 * work,
    )
    terms = exchanged(terms, NEAR)
    (source_grad,) = call(
        source_kernel,
        [((width, rows), f32)],
        (),
        (left_grad, lhs),
        work,
    )
    (terms,) = call(pass_on_kernel, [((len(far),) + piece, bf16)], (), (terms,), 10**5)
    received, terms = lax.optimization_barrier((received, terms))
    terms = exchanged(terms, FAR)
    new_columns, new_state = call(
        update_kernel,
        [((width, rows), f32), ((1, rows), f32)],
        (),
        (columns, row_state.reshape(1, rows), source_grad, received),
        work // 100,
    )
    new_state, terms = lax.optimization_barrier((new_state, terms))
    scale = 1.0 / math.sqrt(edges * axis_size(AXES))
    (rel_grad,) = call(
        functools.partial(collect_kernel, far, scale), [(relation.shape, f32)], (), (terms,), 10**5
    )
    return (new_columns.T, new_state.reshape(rows), rel_grad)


def solution(mesh):
    group, dom = mesh.devices.shape
    fine = Mesh(mesh.devices.reshape(group // 2, 2, 2, dom // 4, 2), AXES)
    split_rows, split = P(AXES, None), P(AXES)
    in_specs = (split_rows, split, P(), split, split, split, split, split)
    out_specs = (split_rows, split, P())
    return jax.shard_map(
        on_device, mesh=fine, in_specs=in_specs, out_specs=out_specs, check_vma=False
    )
```

```python
import functools
import math

import jax
import jax.numpy as jnp
import numpy as np
from jax import lax
from jax.experimental import pallas as pl
from jax.experimental.pallas import tpu as pltpu
from jax.sharding import Mesh
from jax.sharding import PartitionSpec as P

BLOCK = 128
NEG = 512
AXES = ("y", "x_hi", "x_lo", "z", "core")
NEAR = ("x_hi", "x_lo", "z", "core")
FAR = ("y", "x_lo", "core")
PIECE = 128
TILE = 256
WIDE = 1024
CUT = 768
LOG_TWO = 0.6931471805599453
NEVER = -1e30

learn_rate = 0.1

NN = (((1,), (0,)), ((), ()))
NT = (((1,), (1,)), ((), ()))
TN = (((0,), (0,)), ((), ()))


def axis_size(axes):
    return lax.axis_size(axes)


def swapped(x):
    return lax.ppermute(x, "y", [(i, i ^ 1) for i in range(lax.axis_size("y"))])


def exchanged(terms, axes):
    return lax.all_to_all(terms, axes, 0, 0)


def pieces(axes):
    place = np.indices([axis_size(axis) for axis in axes]).reshape(len(axes), -1)
    return [int(k) for k in place[axes.index("x_lo")] * 2 + place[axes.index("core")]]


def dot(a, b, dims):
    return lax.dot_general(a, b, dims, preferred_element_type=jnp.float32)


def one_hot(index, classes):
    row = lax.broadcasted_iota(jnp.int32, (classes, index.shape[1]), 0)
    return (row == index).astype(jnp.float32)


def prepare_kernel(starts, live, embed, embed_rest, relation, lhs, rhs, kinds, source, rel_rows, query, query_rows, bias, target, target_grad):
    cut, rows, edges = embed.shape[1], target.shape[1], lhs.shape[1]
    rel_rows[...] = lax.dot_general(
        relation[...],
        one_hot(kinds[...], relation.shape[0]),
        TN,
        precision=lax.Precision.HIGHEST,
        preferred_element_type=jnp.float32,
    )
    for at in range(0, edges, TILE):
        here = slice(at, at + TILE)
        left_hot = one_hot(lhs[:, here], rows).astype(jnp.bfloat16)
        source_here = dot(embed[...], left_hot[:cut, :], NN) + dot(embed_rest[...], left_hot[cut:, :], NN)
        query_here = source_here * rel_rows[:, here]
        source[:, here] = source_here.astype(jnp.bfloat16)
        query[:, here] = query_here.astype(jnp.bfloat16)
        query_rows[here, :] = query_here.T.astype(jnp.bfloat16)
    row = lax.broadcasted_iota(jnp.int32, (BLOCK, rows), 1)
    for block in range(edges // BLOCK):
        here = slice(block * BLOCK, (block + 1) * BLOCK)
        index = jnp.broadcast_to(rhs[:, here].astype(jnp.float32), (BLOCK, BLOCK)).T
        index = jnp.concatenate([index] * (rows // BLOCK), axis=1).astype(jnp.int32)
        slot = lax.broadcasted_iota(jnp.int32, (BLOCK, rows), 0) + block * BLOCK
        is_target = row == index
        begin = starts[block]
        in_window = (row >= begin) & (row < begin + NEG)
        bias[here, :] = jnp.where(
            in_window, jnp.where(is_target, LOG_TWO, 0.0), jnp.where(is_target, 0.0, NEVER)
        )
        target[here, :] = jnp.where(is_target & (slot < live[0]), 1.0, 0.0).astype(jnp.bfloat16)
    target_grad[...] = -dot(query[...], target[...], NN)


def first_kernel(other, query_rows, bias, target, power, top, total, positives, negatives):
    edges, cut = bias.shape[0], other.shape[1]
    for at in range(0, edges, TILE):
        here = slice(at, at + TILE)
        score = dot(query_rows[here, :], other[...], NN) + bias[here, :cut]
        top_here = jnp.max(score, axis=1, keepdims=True)
        power_here = jnp.exp(score - top_here)
        power[here, :] = power_here
        top[here, :] = top_here
        total[here, :] = jnp.sum(power_here, axis=1, keepdims=True)
        positives[:, here] = dot(other[...], target[here, :cut], NT)
        negatives[:, here] = dot(other[...], power_here.astype(jnp.bfloat16), NT)


def second_kernel(
    live, rest, query, query_rows, bias, target_grad, power, top, total, softmax, sent_grad, scales
):
    edges, cut = power.shape
    for at in range(0, edges, TILE):
        here = slice(at, at + TILE)
        score = dot(query_rows[here, :], rest[...], NN) + bias[here, cut:]
        top_here = jnp.maximum(jnp.max(score, axis=1, keepdims=True), top[here, :])
        power_here = jnp.exp(score - top_here)
        scale = jnp.exp(top[here, :] - top_here)
        total_here = jnp.sum(power_here, axis=1, keepdims=True) + total[here, :] * scale
        slot = lax.broadcasted_iota(jnp.int32, total_here.shape, 0) + at
        weight = jnp.where(slot < live[0], 1.0, 0.0) / total_here
        scale = scale * weight
        scales[:, here] = jnp.broadcast_to(scale, (TILE, BLOCK)).T[:1, :]
        softmax[here, :cut] = (power[here, :] * scale).astype(jnp.bfloat16)
        softmax[here, cut:] = (power_here * weight).astype(jnp.bfloat16)
    sent_grad[...] = (target_grad[...] + dot(query[...], softmax[...], NN)).astype(jnp.bfloat16)


def relation_kernel(
    near_pieces, rest, softmax, target, positives, negatives, scales, source, rel_rows, kinds, left_grad, terms
):
    edges, cut = softmax.shape[0], softmax.shape[1] - rest.shape[1]
    part = jnp.zeros((source.shape[0], terms.shape[1]), jnp.float32)
    for at in range(0, edges, WIDE):
        here = slice(at, at + WIDE)
        dquery = (
            negatives[:, here] * scales[:, here]
            - positives[:, here]
            + dot(rest[...], softmax[here, cut:], NT)
            - dot(rest[...], target[here, cut:], NT)
        )
        kind_hot = one_hot(kinds[:, here], part.shape[1]).astype(jnp.bfloat16)
        change = (dquery * source[:, here].astype(jnp.float32)).astype(jnp.bfloat16)
        part = part + dot(change, kind_hot, NT)
        left_grad[:, here] = (dquery * rel_rows[:, here]).astype(jnp.bfloat16)
    part = part.T
    part = jnp.concatenate([part, jnp.zeros((part.shape[0], -part.shape[1] % PIECE), part.dtype)], axis=1)
    part = part.astype(terms.dtype)
    for k, piece in enumerate(near_pieces):
        terms[k] = part[:, piece * PIECE : (piece + 1) * PIECE]


def pass_on_kernel(terms, summed):
    total = terms[0].astype(jnp.float32)
    for k in range(1, terms.shape[0]):
        total = total + terms[k].astype(jnp.float32)
    total = total.astype(summed.dtype)
    for k in range(summed.shape[0]):
        summed[k] = total


def collect_kernel(far_pieces, scale, terms, rel_grad):
    width = rel_grad.shape[1]
    total = {}
    for k, piece in enumerate(far_pieces):
        term = terms[k].astype(jnp.float32)
        total[piece] = total[piece] + term if piece in total else term
    for piece, term in total.items():
        end = min(width, (piece + 1) * PIECE)
        rel_grad[:, piece * PIECE : end] = term[:, : end - piece * PIECE] * scale


def source_kernel(left_grad, lhs, source_grad):
    edges, rows = lhs.shape[1], source_grad.shape[1]
    grad = jnp.zeros(source_grad.shape, jnp.float32)
    for at in range(0, edges, TILE):
        here = slice(at, at + TILE)
        grad = grad + dot(left_grad[:, here], one_hot(lhs[:, here], rows).astype(jnp.bfloat16), NT)
    source_grad[...] = grad


def update_kernel(slab, state, source_grad, received, new_slab, new_state):
    grad = source_grad[...] + received[...].astype(jnp.float32)
    total = state[...] + jnp.sum(grad * grad, axis=0, keepdims=True) * (1.0 / grad.shape[0])
    new_state[...] = total
    new_slab[...] = slab[...] - grad * (learn_rate / jnp.sqrt(total))


def call(kernel, outs, scalars, vectors, flops, scratch=()):
    scalar = pl.BlockSpec(memory_space=pltpu.SMEM)
    vector = pl.BlockSpec(memory_space=pltpu.VMEM)
    return pl.pallas_call(
        kernel,
        out_shape=[jax.ShapeDtypeStruct(shape, dtype) for shape, dtype in outs],
        in_specs=[scalar] * len(scalars) + [vector] * len(vectors),
        out_specs=[vector] * len(outs),
        scratch_shapes=[pltpu.VMEM(shape, dtype) for shape, dtype in scratch],
        compiler_params=pltpu.CompilerParams(vmem_limit_bytes=24 * 2**20),
        cost_estimate=pl.CostEstimate(flops=flops, bytes_accessed=8 * 2**20, transcendentals=0),
    )(*scalars, *vectors)


def on_device(slab, row_state, relation, lhs_rows, rhs_rows, rel_ids, neg_start, live_edges):
    rows, width = slab.shape
    edges = lhs_rows.shape[0]
    bf16, f32 = jnp.bfloat16, jnp.float32
    columns = slab.T
    embed = columns[:, :CUT].astype(bf16)
    other = swapped(embed)
    embed, later = lax.optimization_barrier((embed, columns[:, CUT:]))
    embed_rest = later.astype(bf16)
    rest = swapped(embed_rest)
    lhs, rhs, kinds = (x.reshape(1, edges) for x in (lhs_rows, rhs_rows, rel_ids))
    work = 2 * rows * edges * width
    source, rel_rows, query, query_rows, bias, target, target_grad = call(
        prepare_kernel,
        [
            ((width, edges), bf16),
            ((width, edges), f32),
            ((width, edges), bf16),
            ((edges, width), bf16),
            ((edges, rows), f32),
            ((edges, rows), bf16),
            ((width, rows), f32),
        ],
        (neg_start, live_edges),
        (embed, embed_rest, relation, lhs, rhs, kinds),
        2 * work,
    )
    power, top, total, positives, negatives = call(
        first_kernel,
        [((edges, CUT), f32), ((edges, 1), f32), ((edges, 1), f32)] + [((width, edges), f32)] * 2,
        (),
        (other, query_rows, bias, target),
        work,
    )
    softmax, sent_grad, scales = call(
        second_kernel,
        [((edges, rows), bf16), ((width, rows), bf16), ((1, edges), f32)],
        (live_edges,),
        (rest, query, query_rows, bias, target_grad, power, top, total),
        2 * work,
    )
    received = swapped(sent_grad)
    near, far = pieces(NEAR), pieces(FAR)
    piece = (relation.shape[0], PIECE)
    left_grad, terms = call(
        functools.partial(relation_kernel, near),
        [((width, edges), bf16), ((len(near),) + piece, bf16)],
        (),
        (rest, softmax, target, positives, negatives, scales, source, rel_rows, kinds),
        2 * work,
    )
    terms = exchanged(terms, NEAR)
    (source_grad,) = call(
        source_kernel,
        [((width, rows), f32)],
        (),
        (left_grad, lhs),
        work,
    )
    (terms,) = call(pass_on_kernel, [((len(far),) + piece, bf16)], (), (terms,), 10**5)
    received, terms = lax.optimization_barrier((received, terms))
    terms = exchanged(terms, FAR)
    new_columns, new_state = call(
        update_kernel,
        [((width, rows), f32), ((1, rows), f32)],
        (),
        (columns, row_state.reshape(1, rows), source_grad, received),
        work // 100,
    )
    new_state, terms = lax.optimization_barrier((new_state, terms))
    scale = 1.0 / math.sqrt(edges * axis_size(AXES))
    (rel_grad,) = call(
        functools.partial(collect_kernel, far, scale), [(relation.shape, f32)], (), (terms,), 10**5
    )
    return (new_columns.T, new_state.reshape(rows), rel_grad)


def solution(mesh):
    group, dom = mesh.devices.shape
    fine = Mesh(mesh.devices.reshape(group // 2, 2, 2, dom // 4, 2), AXES)
    split_rows, split = P(AXES, None), P(AXES)
    in_specs = (split_rows, split, P(), split, split, split, split, split)
    out_specs = (split_rows, split, P())
    return jax.shard_map(
        on_device, mesh=fine, in_specs=in_specs, out_specs=out_specs, check_vma=False
    )
```

```python
import functools
import math

import jax
import jax.numpy as jnp
import numpy as np
from jax import lax
from jax.experimental import pallas as pl
from jax.experimental.pallas import tpu as pltpu
from jax.sharding import Mesh
from jax.sharding import PartitionSpec as P

BLOCK = 128
NEG = 512
AXES = ("y", "x_hi", "x_lo", "z", "core")
NEAR = ("x_hi", "x_lo", "z", "core")
FAR = ("y", "x_lo", "core")
PIECE = 128
TILE = 256
HALF = 512
WIDE = 1024
CUT = 768
LOG_TWO = 0.6931471805599453
NEVER = -1e30

learn_rate = 0.1

NN = (((1,), (0,)), ((), ()))
NT = (((1,), (1,)), ((), ()))
TN = (((0,), (0,)), ((), ()))


def axis_size(axes):
    return lax.axis_size(axes)


def swapped(x):
    return lax.ppermute(x, "y", [(i, i ^ 1) for i in range(lax.axis_size("y"))])


def exchanged(terms, axes):
    return lax.all_to_all(terms, axes, 0, 0)


def pieces(axes):
    place = np.indices([axis_size(axis) for axis in axes]).reshape(len(axes), -1)
    return [int(k) for k in place[axes.index("x_lo")] * 2 + place[axes.index("core")]]


def dot(a, b, dims):
    return lax.dot_general(a, b, dims, preferred_element_type=jnp.float32)


def one_hot(index, classes):
    row = lax.broadcasted_iota(jnp.int32, (classes, index.shape[1]), 0)
    return (row == index).astype(jnp.float32)


def prepare_kernel(starts, live, embed, embed_rest, relation, lhs, rhs, kinds, source, rel_rows, query, query_rows, bias, target, target_grad):
    cut, rows, edges = embed.shape[1], target.shape[1], lhs.shape[1]
    rel_rows[...] = lax.dot_general(
        relation[...],
        one_hot(kinds[...], relation.shape[0]),
        TN,
        precision=lax.Precision.HIGHEST,
        preferred_element_type=jnp.float32,
    )
    for at in range(0, edges, TILE):
        here = slice(at, at + TILE)
        left_hot = one_hot(lhs[:, here], rows).astype(jnp.bfloat16)
        source_here = dot(embed[...], left_hot[:cut, :], NN) + dot(embed_rest[...], left_hot[cut:, :], NN)
        query_here = source_here * rel_rows[:, here]
        source[:, here] = source_here.astype(jnp.bfloat16)
        query[:, here] = query_here.astype(jnp.bfloat16)
        query_rows[here, :] = query_here.T.astype(jnp.bfloat16)
    row = lax.broadcasted_iota(jnp.int32, (BLOCK, rows), 1)
    for block in range(edges // BLOCK):
        here = slice(block * BLOCK, (block + 1) * BLOCK)
        index = jnp.broadcast_to(rhs[:, here].astype(jnp.float32), (BLOCK, BLOCK)).T
        index = jnp.concatenate([index] * (rows // BLOCK), axis=1).astype(jnp.int32)
        slot = lax.broadcasted_iota(jnp.int32, (BLOCK, rows), 0) + block * BLOCK
        is_target = row == index
        begin = starts[block]
        in_window = (row >= begin) & (row < begin + NEG)
        bias[here, :] = jnp.where(
            in_window, jnp.where(is_target, LOG_TWO, 0.0), jnp.where(is_target, 0.0, NEVER)
        )
        target[here, :] = jnp.where(is_target & (slot < live[0]), 1.0, 0.0).astype(jnp.bfloat16)
    target_grad[...] = -dot(query[...], target[...], NN)


def first_kernel(other, query_rows, bias, target, power, top, total, positives, negatives):
    edges, cut = bias.shape[0], other.shape[1]
    for at in range(0, edges, HALF):
        here = slice(at, at + HALF)
        score = dot(query_rows[here, :], other[...], NN) + bias[here, :cut]
        top_here = jnp.max(score, axis=1, keepdims=True)
        power_here = jnp.exp(score - top_here)
        power[here, :] = power_here
        top[here, :] = top_here
        total[here, :] = jnp.sum(power_here, axis=1, keepdims=True)
        positives[:, here] = dot(other[...], target[here, :cut], NT)
        negatives[:, here] = dot(other[...], power_here.astype(jnp.bfloat16), NT)


def second_kernel(
    live, rest, query, query_rows, bias, target_grad, power, top, total, softmax, sent_grad, scales
):
    edges, cut = power.shape
    for at in range(0, edges, TILE):
        here = slice(at, at + TILE)
        score = dot(query_rows[here, :], rest[...], NN) + bias[here, cut:]
        top_here = jnp.maximum(jnp.max(score, axis=1, keepdims=True), top[here, :])
        power_here = jnp.exp(score - top_here)
        scale = jnp.exp(top[here, :] - top_here)
        total_here = jnp.sum(power_here, axis=1, keepdims=True) + total[here, :] * scale
        slot = lax.broadcasted_iota(jnp.int32, total_here.shape, 0) + at
        weight = jnp.where(slot < live[0], 1.0, 0.0) / total_here
        scale = scale * weight
        scales[:, here] = jnp.broadcast_to(scale, (TILE, BLOCK)).T[:1, :]
        softmax[here, :cut] = (power[here, :] * scale).astype(jnp.bfloat16)
        softmax[here, cut:] = (power_here * weight).astype(jnp.bfloat16)
    sent_grad[...] = (target_grad[...] + dot(query[...], softmax[...], NN)).astype(jnp.bfloat16)


def relation_kernel(
    near_pieces, rest, softmax, target, positives, negatives, scales, source, rel_rows, kinds, left_grad, terms
):
    edges, cut = softmax.shape[0], softmax.shape[1] - rest.shape[1]
    part = jnp.zeros((source.shape[0], terms.shape[1]), jnp.float32)
    for at in range(0, edges, WIDE):
        here = slice(at, at + WIDE)
        dquery = (
            negatives[:, here] * scales[:, here]
            - positives[:, here]
            + dot(rest[...], softmax[here, cut:], NT)
            - dot(rest[...], target[here, cut:], NT)
        )
        kind_hot = one_hot(kinds[:, here], part.shape[1]).astype(jnp.bfloat16)
        change = (dquery * source[:, here].astype(jnp.float32)).astype(jnp.bfloat16)
        part = part + dot(change, kind_hot, NT)
        left_grad[:, here] = (dquery * rel_rows[:, here]).astype(jnp.bfloat16)
    part = part.T
    part = jnp.concatenate([part, jnp.zeros((part.shape[0], -part.shape[1] % PIECE), part.dtype)], axis=1)
    part = part.astype(terms.dtype)
    for k, piece in enumerate(near_pieces):
        terms[k] = part[:, piece * PIECE : (piece + 1) * PIECE]


def pass_on_kernel(terms, summed):
    total = terms[0].astype(jnp.float32)
    for k in range(1, terms.shape[0]):
        total = total + terms[k].astype(jnp.float32)
    total = total.astype(summed.dtype)
    for k in range(summed.shape[0]):
        summed[k] = total


def collect_kernel(far_pieces, scale, terms, rel_grad):
    width = rel_grad.shape[1]
    total = {}
    for k, piece in enumerate(far_pieces):
        term = terms[k].astype(jnp.float32)
        total[piece] = total[piece] + term if piece in total else term
    for piece, term in total.items():
        end = min(width, (piece + 1) * PIECE)
        rel_grad[:, piece * PIECE : end] = term[:, : end - piece * PIECE] * scale


def source_kernel(left_grad, lhs, source_grad):
    edges, rows = lhs.shape[1], source_grad.shape[1]
    grad = jnp.zeros(source_grad.shape, jnp.float32)
    for at in range(0, edges, TILE):
        here = slice(at, at + TILE)
        grad = grad + dot(left_grad[:, here], one_hot(lhs[:, here], rows).astype(jnp.bfloat16), NT)
    source_grad[...] = grad


def update_kernel(slab, state, source_grad, received, new_slab, new_state):
    grad = source_grad[...] + received[...].astype(jnp.float32)
    total = state[...] + jnp.sum(grad * grad, axis=0, keepdims=True) * (1.0 / grad.shape[0])
    new_state[...] = total
    new_slab[...] = slab[...] - grad * (learn_rate / jnp.sqrt(total))


def call(kernel, outs, scalars, vectors, flops, scratch=()):
    scalar = pl.BlockSpec(memory_space=pltpu.SMEM)
    vector = pl.BlockSpec(memory_space=pltpu.VMEM)
    return pl.pallas_call(
        kernel,
        out_shape=[jax.ShapeDtypeStruct(shape, dtype) for shape, dtype in outs],
        in_specs=[scalar] * len(scalars) + [vector] * len(vectors),
        out_specs=[vector] * len(outs),
        scratch_shapes=[pltpu.VMEM(shape, dtype) for shape, dtype in scratch],
        compiler_params=pltpu.CompilerParams(vmem_limit_bytes=24 * 2**20),
        cost_estimate=pl.CostEstimate(flops=flops, bytes_accessed=8 * 2**20, transcendentals=0),
    )(*scalars, *vectors)


def on_device(slab, row_state, relation, lhs_rows, rhs_rows, rel_ids, neg_start, live_edges):
    rows, width = slab.shape
    edges = lhs_rows.shape[0]
    bf16, f32 = jnp.bfloat16, jnp.float32
    columns = slab.T
    embed = columns[:, :CUT].astype(bf16)
    other = swapped(embed)
    embed, later = lax.optimization_barrier((embed, columns[:, CUT:]))
    embed_rest = later.astype(bf16)
    rest = swapped(embed_rest)
    lhs, rhs, kinds = (x.reshape(1, edges) for x in (lhs_rows, rhs_rows, rel_ids))
    work = 2 * rows * edges * width
    source, rel_rows, query, query_rows, bias, target, target_grad = call(
        prepare_kernel,
        [
            ((width, edges), bf16),
            ((width, edges), f32),
            ((width, edges), bf16),
            ((edges, width), bf16),
            ((edges, rows), f32),
            ((edges, rows), bf16),
            ((width, rows), f32),
        ],
        (neg_start, live_edges),
        (embed, embed_rest, relation, lhs, rhs, kinds),
        2 * work,
    )
    power, top, total, positives, negatives = call(
        first_kernel,
        [((edges, CUT), f32), ((edges, 1), f32), ((edges, 1), f32)] + [((width, edges), f32)] * 2,
        (),
        (other, query_rows, bias, target),
        work,
    )
    softmax, sent_grad, scales = call(
        second_kernel,
        [((edges, rows), bf16), ((width, rows), bf16), ((1, edges), f32)],
        (live_edges,),
        (rest, query, query_rows, bias, target_grad, power, top, total),
        2 * work,
    )
    received = swapped(sent_grad)
    near, far = pieces(NEAR), pieces(FAR)
    piece = (relation.shape[0], PIECE)
    left_grad, terms = call(
        functools.partial(relation_kernel, near),
        [((width, edges), bf16), ((len(near),) + piece, bf16)],
        (),
        (rest, softmax, target, positives, negatives, scales, source, rel_rows, kinds),
        2 * work,
    )
    terms = exchanged(terms, NEAR)
    (source_grad,) = call(
        source_kernel,
        [((width, rows), f32)],
        (),
        (left_grad, lhs),
        work,
    )
    (terms,) = call(pass_on_kernel, [((len(far),) + piece, bf16)], (), (terms,), 10**5)
    received, terms = lax.optimization_barrier((received, terms))
    terms = exchanged(terms, FAR)
    new_columns, new_state = call(
        update_kernel,
        [((width, rows), f32), ((1, rows), f32)],
        (),
        (columns, row_state.reshape(1, rows), source_grad, received),
        work // 100,
    )
    new_state, terms = lax.optimization_barrier((new_state, terms))
    scale = 1.0 / math.sqrt(edges * axis_size(AXES))
    (rel_grad,) = call(
        functools.partial(collect_kernel, far, scale), [(relation.shape, f32)], (), (terms,), 10**5
    )
    return (new_columns.T, new_state.reshape(rows), rel_grad)


def solution(mesh):
    group, dom = mesh.devices.shape
    fine = Mesh(mesh.devices.reshape(group // 2, 2, 2, dom // 4, 2), AXES)
    split_rows, split = P(AXES, None), P(AXES)
    in_specs = (split_rows, split, P(), split, split, split, split, split)
    out_specs = (split_rows, split, P())
    return jax.shard_map(
        on_device, mesh=fine, in_specs=in_specs, out_specs=out_specs, check_vma=False
    )
```
